256 devices in a mesh: row: 64 (over y_hi, x, z), fit: 4 (over y_lo, core).
Axes of the slice: x: 4, y: 4 (y_hi: 2, y_lo: 2; y = y_hi * 2 + y_lo), z: 8, core: 2. Of those that a mesh axis runs over, the one named last changes fastest.
Arguments:
- blocks: bfloat16 [9728, 8, 1200], P('row', 'fit'), may hold values from -0.59765625 to 0.59765625
Outputs:
- exchange_matrix: float32 [9728, 9728], P(('row', 'fit'))
The draws below stay inside these ranges and needn't reach their ends.
All inputs are finite; a program needn't handle non-finite values.
Results may differ from the reference program's by a relative error of at most 0.0003.
Values may be sent and summed in bfloat16 or wider, within the bound.
No kernel may reach another device: no remote copies, remote signals or barrier semaphores. Data moves between devices by JAX's collectives and lax.ppermute only.
A program may use at most 128 MiB of HBM per device.

```python
import jax
import jax.numpy as jnp
from jax import lax

NBF = 9728
OCC = 1200
NAUX = 8


def levels(stream_key, dims, shards, least, top_value):
    loudness, own = 1.0, jax.random.fold_in(stream_key, 6)
    for position, blocks in shards:
        steps = jnp.exp(jax.random.uniform(jax.random.fold_in(own, position), (blocks,), jnp.float32, least / len(shards), top_value / len(shards)))
        loudness = loudness * jnp.repeat(steps, dims[position] // blocks).reshape([-1 if axis == position else 1 for axis in range(len(dims))])
    return loudness


def normal_values(rng, dims, deviation, limit, split=(), held_as=jnp.bfloat16):
    factor_of = levels(rng, dims, split, -0.22, 0.18) if split else 1.0
    values = jax.random.normal(rng, dims, jnp.float32) * deviation * factor_of
    return jnp.minimum(jnp.maximum(values, -limit), limit).astype(held_as)


def setup_inputs(seed: int = 0) -> dict:
    key_list = jax.random.split(jax.random.key(seed), 2)
    blocks = normal_values(key_list[0], (NBF, NAUX, OCC), 0.08, 0.59765625, ((0, 64), (1, 4)))
    return {"blocks": blocks}


def reference(blocks):
    flat = blocks.astype(jnp.float32).reshape(NBF, NAUX * OCC)
    return jnp.dot(flat, flat.T, precision=lax.Precision.HIGHEST, preferred_element_type=jnp.float32)
```

```python
import jax
import jax.numpy as jnp
from jax import lax
from jax.sharding import Mesh
from jax.sharding import PartitionSpec as P

ROWS = 152
DEPTH = 2400
PIECE = 38
PADDED = 40


def shift(value, axis, by, size):
    return lax.ppermute(value, axis, [(i, (i + by) % size) for i in range(size)])


def across(value):
    return lax.ppermute(value, ("yh", "yl"), [(0, 3), (1, 2), (2, 1), (3, 0)])


def ring_of_four(value):
    ahead = shift(value, "x", -1, 4)
    behind = shift(value, "x", 1, 4)
    half = value.shape[0] // 2
    far = jnp.concatenate([shift(ahead[:half], "x", -1, 4), shift(behind[half:], "x", 1, 4)], axis=0)
    return [value, ahead, far, behind]


def ring_of_eight(value):
    ahead, behind = [value], [value]
    for _ in range(3):
        ahead.append(shift(ahead[-1], "z", -1, 8))
        behind.append(shift(behind[-1], "z", 1, 8))
    far = jnp.concatenate([shift(ahead[-1][:80], "z", -1, 8), shift(behind[-1][80:], "z", 1, 8)], axis=0)
    return ahead + [far] + behind[:0:-1]


def dot(left, right):
    return lax.dot_general(left, right, (((1,), (1,)), ((), ())), preferred_element_type=jnp.float32)


def on_device(blocks):
    core, yl = lax.axis_index("c"), lax.axis_index("yl")
    yh, x, z = lax.axis_index("yh"), lax.axis_index("x"), lax.axis_index("z")
    own = blocks.reshape(ROWS, DEPTH)
    line = ring_of_eight(own)
    line_other = [shift(block, "c", 1, 2) for block in line]

    def pieces(block):
        split = jnp.pad(block.reshape(2, 2, PIECE, DEPTH), ((0, 0), (0, 0), (0, PADDED - PIECE), (0, 0)))
        return lax.dynamic_index_in_dim(split, core, 1, keepdims=False)

    mine = jnp.stack([pieces(own), pieces(line_other[0])])
    mine = jnp.swapaxes(mine, 0, 1)
    plane = ring_of_four(mine) + ring_of_four(shift(mine, "yh", 1, 2))
    plane = jnp.stack(plane, axis=0)
    left = [jnp.swapaxes(plane[:, :, s], 0, 1).reshape(2 * 8 * PADDED, DEPTH) for s in range(2)]
    right = [jnp.concatenate(line), jnp.concatenate(line_other)]
    partial = dot(left[0], right[0]) + dot(left[1], right[1])
    partial = partial.reshape(2, 2, 4 * PADDED, 8 * ROWS)
    near, far = partial[:, 0], partial[:, 1]
    kept_near = lax.dynamic_index_in_dim(near, yl, 0, keepdims=False)
    sent_near = lax.dynamic_index_in_dim(near, 1 - yl, 0, keepdims=False)
    kept_far = lax.dynamic_index_in_dim(far, 1 - yl, 0, keepdims=False)
    sent_far = lax.dynamic_index_in_dim(far, yl, 0, keepdims=False)
    far = across(kept_far + shift(sent_far, "yl", 1, 2))
    near = kept_near + shift(sent_near, "yl", 1, 2)
    both = jnp.stack([near, far]).reshape(2, 4, PADDED, 8 * ROWS)
    arrived = jnp.stack(
        [
            both[:, 0],
            shift(both[:, 1], "x", 1, 4),
            shift(both[:, 2], "x", 2, 4),
            shift(both[:, 3], "x", 3, 4),
        ],
        axis=1,
    )
    arrived = arrived[:, :, :PIECE].reshape(2, 4, PIECE, 8, ROWS)
    arrived = jnp.take(arrived, (jnp.arange(2) + yh) % 2, axis=0)
    arrived = jnp.take(arrived, (x - jnp.arange(4)) % 4, axis=1)
    arrived = jnp.take(arrived, (jnp.arange(8) - z) % 8, axis=3)
    return jnp.transpose(arrived, (2, 0, 1, 3, 4)).reshape(PIECE, 64 * ROWS)


def solution(mesh):
    finer = Mesh(mesh.devices.reshape(2, 4, 8, 2, 2), ("yh", "x", "z", "yl", "c"))
    return jax.shard_map(
        on_device,
        mesh=finer,
        in_specs=(P(("yh", "x", "z"), ("yl", "c"), None),),
        out_specs=P(("yh", "x", "z", "yl", "c"), None),
        check_vma=False,
    )
```

```python
import functools

import jax
import jax.numpy as jnp
from jax import lax
from jax.experimental import pallas as pl
from jax.experimental.pallas import tpu as pltpu
from jax.sharding import Mesh
from jax.sharding import PartitionSpec as P

ROWS = 152
DEPTH = 2400
PIECE = 38
PADDED = 40
HALF = 2 * PADDED
GROUPS = ((0, 1, 7, 2, 6), (3, 4, 5))


def shift(value, axis, by):
    size = lax.axis_size(axis)
    return lax.ppermute(value, axis, [(i, (i + by) % size) for i in range(size)])


def across(value):
    return lax.ppermute(value, ("yh", "yl"), [(0, 3), (1, 2), (2, 1), (3, 0)])


def dot(left, right):
    return lax.dot_general(left, right, (((1,), (1,)), ((), ())), preferred_element_type=jnp.float32)


def assemble_kernel(place, *refs):
    *parts, out, held = refs
    yh, x, z = place[0], place[1], place[2]
    for g, group in enumerate(GROUPS):
        for y in range(2):
            for d in range(4):
                for j, a in enumerate(group):
                    held[y * 4 + d, a, :, :ROWS] = parts[g * 4 + d][y, :, j * ROWS : (j + 1) * ROWS]
    for y in range(2):
        for i in range(4):
            source = lax.rem(y + yh, 2) * 4 + lax.rem(x - i + 4, 4)
            for a in range(8):
                at = ((y * 4 + i) * 8 + a) * ROWS
                out[:, at : at + ROWS] = held[source, lax.rem(a - z + 8, 8), :PIECE, :ROWS]


def assemble(place, parts):
    return pl.pallas_call(
        assemble_kernel,
        out_shape=jax.ShapeDtypeStruct((PIECE, 64 * ROWS), jnp.float32),
        in_specs=[pl.BlockSpec(memory_space=pltpu.SMEM)] + [pl.BlockSpec(memory_space=pltpu.VMEM)] * len(parts),
        out_specs=pl.BlockSpec(memory_space=pltpu.VMEM),
        scratch_shapes=[pltpu.VMEM((8, 8, PADDED, 256), jnp.float32)],
        compiler_params=pltpu.CompilerParams(vmem_limit_bytes=16 * 1024 * 1024),
    )(place, *parts)


def hold(*values):
    return lax.optimization_barrier(values)


def owner_order_kernel(place, *refs):
    *slices, out = refs
    yl, core = place[3], place[4]
    for k, rows in enumerate(slices):
        for y in range(2):
            slot = 2 * k + jnp.where(yl == y, 1, 0)
            for c in range(2):

                @pl.when(core == c)
                def _(at=(y * 2 + c) * PIECE):
                    out[slot, :PIECE] = rows[at : at + PIECE]

            out[slot, PIECE:] = jnp.zeros((PADDED - PIECE, DEPTH), rows.dtype)


def owner_order(place, *slices):
    return pl.pallas_call(
        owner_order_kernel,
        out_shape=jax.ShapeDtypeStruct((4, PADDED, DEPTH), slices[0].dtype),
        in_specs=[pl.BlockSpec(memory_space=pltpu.SMEM)] + [pl.BlockSpec(memory_space=pltpu.VMEM)] * 2,
        out_specs=pl.BlockSpec(memory_space=pltpu.VMEM),
        compiler_params=pltpu.CompilerParams(vmem_limit_bytes=12 * 1024 * 1024),
    )(place, *slices)


def left_rows(blocks, halves):
    pieces = [block.reshape(2, 2, PADDED, DEPTH) for block in blocks]
    return [jnp.concatenate([piece[k, half] for half in halves for piece in pieces]) for k in range(2)]


def product(left, right):
    total = dot(left[0], right[0]) + dot(left[1], right[1])
    return total[: 4 * PADDED], total[4 * PADDED :]


def both_cores(*blocks):
    joined = shift(jnp.concatenate(blocks), "c", 1)
    return [joined[i * ROWS : (i + 1) * ROWS] for i in range(len(blocks))]


def to_owner_x(near, far):
    both = jnp.stack([near, far]).reshape(2, 4, PADDED, -1)
    return [both[:, 0]] + [shift(both[:, d], "x", d) for d in range(1, 4)]


def on_device(blocks):
    place = jnp.stack([lax.axis_index(name) for name in ("yh", "x", "z", "yl", "c")]).astype(jnp.int32)
    own = blocks.reshape(ROWS, DEPTH)
    z1, z7 = shift(own, "z", -1), shift(own, "z", 1)
    (own_,) = both_cores(own)
    mine = owner_order(place, own, own_).reshape(4 * PADDED, DEPTH)

    x1, x3, other = shift(mine, "x", -1), shift(mine, "x", 1), shift(mine, "yh", 1)
    z1, z7, x1, x3, other = hold(z1, z7, x1, x3, other)

    z2, z6 = shift(z1, "z", -1), shift(z7, "z", 1)
    ahead = shift(jnp.concatenate([x1[:HALF], other[HALF:]]), "x", -1)
    behind = shift(jnp.concatenate([other[:HALF], x3[HALF:]]), "x", 1)
    yh = shift(jnp.concatenate([x1[:HALF], x3[HALF:]]), "yh", 1)
    z2, z6, ahead, behind, yh = hold(z2, z6, ahead, behind, yh)

    z3, z5 = shift(z2, "z", -1), shift(z6, "z", 1)
    o2_low, o2_high = shift(yh[:HALF], "x", -1), shift(yh[HALF:], "x", 1)
    first = jnp.concatenate([z1, z7, z2, z6])
    first_ = shift(first, "c", 1)
    x2 = jnp.concatenate([ahead[:HALF], behind[HALF:]])
    o1 = jnp.concatenate([yh[:HALF], ahead[HALF:]])
    o3 = jnp.concatenate([behind[:HALF], yh[HALF:]])
    near = left_rows((mine, x1, x2, x3), (0, 1))
    z3, z5, o2_low, o2_high, first_, *near = hold(z3, z5, o2_low, o2_high, first_, *near)
    far = left_rows((other, o1, jnp.concatenate([o2_low, o2_high]), o3), (1, 0))
    first = [jnp.concatenate([own, first]), jnp.concatenate([own_, first_])]
    f1, f1_kept = product(far, first)
    f1, near, first = hold(f1, tuple(near), tuple(first))

    f1 = shift(f1, "yl", 1)
    z4_low, z4_high = shift(z3[:80], "z", -1), shift(z5[80:], "z", 1)
    z3_, z5_ = both_cores(z3, z5)
    n1, n1_kept = product(near, first)
    f1, n1, z3_, z5_ = hold(f1, n1, z3_, z5_)
    f1 = across(f1_kept + f1)
    n1 = shift(n1, "yl", 1)
    z4_low, z4_high = hold(z4_low, z4_high)
    z4 = jnp.concatenate([z4_low, z4_high])
    (z4_,) = both_cores(z4)
    last = [jnp.concatenate([z3, z4, z5]), jnp.concatenate([z3_, z4_, z5_])]
    f2, f2_kept = product(far, last)
    n2, n2_kept = product(near, last)
    n1, f1, f2, n2 = hold(n1, f1, f2, n2)
    f2 = shift(f2, "yl", 1)
    parts = to_owner_x(n1_kept + n1, f1)
    f2, n2 = hold(f2, n2)
    f2 = across(f2_kept + f2)
    n2 = shift(n2, "yl", 1)
    f2, n2, *parts = hold(f2, n2, *parts)
    parts += to_owner_x(n2_kept + n2, f2)
    return assemble(place, parts)


def solution(mesh):
    finer = Mesh(mesh.devices.reshape(2, 4, 8, 2, 2), ("yh", "x", "z", "yl", "c"))
    return jax.shard_map(
        on_device,
        mesh=finer,
        in_specs=(P(("yh", "x", "z"), ("yl", "c"), None),),
        out_specs=P(("yh", "x", "z", "yl", "c"), None),
        check_vma=False,
    )
```

```python
import functools

import jax
import jax.numpy as jnp
from jax import lax
from jax.experimental import pallas as pl
from jax.experimental.pallas import tpu as pltpu
from jax.sharding import Mesh
from jax.sharding import PartitionSpec as P

ROWS = 152
DEPTH = 2400
PIECE = 38
PADDED = 40
HALF = 2 * PADDED
GROUPS = ((0, 1, 7, 2, 6), (3, 4, 5))


def shift(value, axis, by):
    size = lax.axis_size(axis)
    return lax.ppermute(value, axis, [(i, (i + by) % size) for i in range(size)])


def across(value):
    return lax.ppermute(value, ("yh", "yl"), [(0, 3), (1, 2), (2, 1), (3, 0)])


def dot(left, right):
    return lax.dot_general(left, right, (((1,), (1,)), ((), ())), preferred_element_type=jnp.float32)


def assemble_kernel(place, *refs):
    *parts, out, held = refs
    yh, x, z = place[0], place[1], place[2]
    for d in range(4):
        for y in range(2):
            for part, at, group in ((parts[y * 4 + d], 0, GROUPS[0]), (parts[8 + d], y * PADDED, GROUPS[1])):
                for j, a in enumerate(group):
                    held[y * 4 + d, a, :, :ROWS] = part[at : at + PADDED, j * ROWS : (j + 1) * ROWS]
    for y in range(2):
        for i in range(4):
            source = lax.rem(y + yh, 2) * 4 + lax.rem(x - i + 4, 4)
            for a in range(8):
                at = ((y * 4 + i) * 8 + a) * ROWS
                out[:, at : at + ROWS] = held[source, lax.rem(a - z + 8, 8), :PIECE, :ROWS]


def assemble(place, parts):
    return pl.pallas_call(
        assemble_kernel,
        out_shape=jax.ShapeDtypeStruct((PIECE, 64 * ROWS), jnp.float32),
        in_specs=[pl.BlockSpec(memory_space=pltpu.SMEM)] + [pl.BlockSpec(memory_space=pltpu.VMEM)] * len(parts),
        out_specs=pl.BlockSpec(memory_space=pltpu.VMEM),
        scratch_shapes=[pltpu.VMEM((8, 8, PADDED, 256), jnp.float32)],
        compiler_params=pltpu.CompilerParams(vmem_limit_bytes=16 * 1024 * 1024),
    )(place, *parts)


def hold(*values):
    return lax.optimization_barrier(values)


def owner_order_kernel(place, *refs):
    *slices, out = refs
    yl, core = place[3], place[4]
    for k, rows in enumerate(slices):
        for y in range(2):
            slot = 2 * k + jnp.where(yl == y, 1, 0)
            for c in range(2):

                @pl.when(core == c)
                def _(at=(y * 2 + c) * PIECE):
                    out[slot, :PIECE] = rows[at : at + PIECE]

            out[slot, PIECE:] = jnp.zeros((PADDED - PIECE, DEPTH), rows.dtype)


def owner_order(place, *slices):
    return pl.pallas_call(
        owner_order_kernel,
        out_shape=jax.ShapeDtypeStruct((4, PADDED, DEPTH), slices[0].dtype),
        in_specs=[pl.BlockSpec(memory_space=pltpu.SMEM)] + [pl.BlockSpec(memory_space=pltpu.VMEM)] * 2,
        out_specs=pl.BlockSpec(memory_space=pltpu.VMEM),
        compiler_params=pltpu.CompilerParams(vmem_limit_bytes=12 * 1024 * 1024),
    )(place, *slices)


def left_rows(blocks, halves):
    pieces = [block.reshape(2, 2, PADDED, DEPTH) for block in blocks]
    return [jnp.concatenate([piece[k, half] for half in halves for piece in pieces]) for k in range(2)]


def product(left, right):
    total = dot(left[0], right[0]) + dot(left[1], right[1])
    return total[: 4 * PADDED], total[4 * PADDED :]


def both_cores(*blocks):
    joined = shift(jnp.concatenate(blocks), "c", 1)
    return [joined[i * ROWS : (i + 1) * ROWS] for i in range(len(blocks))]


def to_owner_x(value):
    rows = value.shape[0] // 4
    return [value[:rows]] + [shift(value[d * rows : (d + 1) * rows], "x", d) for d in range(1, 4)]


def on_device(blocks):
    place = jnp.stack([lax.axis_index(name) for name in ("yh", "x", "z", "yl", "c")]).astype(jnp.int32)
    own = blocks.reshape(ROWS, DEPTH)
    z1, z7 = shift(own, "z", -1), shift(own, "z", 1)
    (own_,) = both_cores(own)
    mine = owner_order(place, own, own_).reshape(4 * PADDED, DEPTH)

    x1, x3, other = shift(mine, "x", -1), shift(mine, "x", 1), shift(mine, "yh", 1)
    z1, z7 = hold(z1, z7)
    z2, z6 = shift(z1, "z", -1), shift(z7, "z", 1)
    x1, x3, other, z1, z7 = hold(x1, x3, other, z1, z7)
    ahead = shift(jnp.concatenate([x1[:HALF], other[HALF:]]), "x", -1)
    behind = shift(jnp.concatenate([other[:HALF], x3[HALF:]]), "x", 1)
    yh = shift(jnp.concatenate([x1[:HALF], x3[HALF:]]), "yh", 1)
    z2, z6, x1, x3 = hold(z2, z6, x1, x3)

    z3, z5 = shift(z2, "z", -1), shift(z6, "z", 1)
    ahead, behind, yh, z2, z6 = hold(ahead, behind, yh, z2, z6)
    o2_low, o2_high = shift(yh[:HALF], "x", -1), shift(yh[HALF:], "x", 1)
    first = jnp.concatenate([z1, z7, z2, z6])
    first_ = shift(first, "c", 1)
    x2 = jnp.concatenate([ahead[:HALF], behind[HALF:]])
    o1 = jnp.concatenate([yh[:HALF], ahead[HALF:]])
    o3 = jnp.concatenate([behind[:HALF], yh[HALF:]])
    near = left_rows((mine, x1, x2, x3), (0, 1))
    first_, *near = hold(first_, *near)
    first = [jnp.concatenate([own, first]), jnp.concatenate([own_, first_])]
    n1, n1_kept = product(near, first)
    z3, z5, n1, near, first = hold(z3, z5, n1, tuple(near), tuple(first))

    n1 = shift(n1, "yl", 1)
    z4_low, z4_high = shift(z3[:80], "z", -1), shift(z5[80:], "z", 1)
    z3_, z5_ = both_cores(z3, z5)
    z3_, z5_, o2_low, o2_high = hold(z3_, z5_, o2_low, o2_high)
    far = left_rows((other, o1, jnp.concatenate([o2_low, o2_high]), o3), (1, 0))
    f1, f1_kept = product(far, first)
    z4_low, z4_high, f1, far = hold(z4_low, z4_high, f1, tuple(far))

    f1 = shift(f1, "yl", 1)
    z4 = jnp.concatenate([z4_low, z4_high])
    (z4_,) = both_cores(z4)
    z3_, z4_, z5_ = hold(z3_, z4_, z5_)
    last = [jnp.concatenate([z3, z4, z5]), jnp.concatenate([z3_, z4_, z5_])]
    f2, f2_kept = product(far, last)
    last, f2 = hold(tuple(last), f2)
    n2, n2_kept = product(near, last)
    n1, f2, n2 = hold(n1, f2, n2)

    n1_parts = to_owner_x(n1_kept + n1)
    f2 = shift(f2, "yl", 1)
    f1, n2, *n1_parts = hold(f1, n2, *n1_parts)

    n2 = shift(n2, "yl", 1)
    f1 = across(f1_kept + f1)
    f2, f1_kept = hold(f2, f1_kept)
    f2 = across(f2_kept + f2)
    f1, f2_kept = hold(f1, f2_kept)
    f1_parts = to_owner_x(f1)
    f2, n2, *f1_parts = hold(f2, n2, *f1_parts)

    second = jnp.concatenate([(n2_kept + n2).reshape(4, PADDED, -1), f2.reshape(4, PADDED, -1)], axis=1)
    second = to_owner_x(second.reshape(8 * PADDED, -1))
    return assemble(place, n1_parts + f1_parts + second)


def solution(mesh):
    finer = Mesh(mesh.devices.reshape(2, 4, 8, 2, 2), ("yh", "x", "z", "yl", "c"))
    return jax.shard_map(
        on_device,
        mesh=finer,
        in_specs=(P(("yh", "x", "z"), ("yl", "c"), None),),
        out_specs=P(("yh", "x", "z", "yl", "c"), None),
        check_vma=False,
    )
```

```python
import functools

import jax
import jax.numpy as jnp
from jax import lax
from jax.experimental import pallas as pl
from jax.experimental.pallas import tpu as pltpu
from jax.sharding import Mesh
from jax.sharding import PartitionSpec as P

ROWS = 152
DEPTH = 2400
PIECE = 38
PADDED = 40
HALF = 2 * PADDED
GROUPS = ((0, 1, 7, 2, 6), (3, 4, 5))


def shift(value, axis, by):
    size = lax.axis_size(axis)
    return lax.ppermute(value, axis, [(i, (i + by) % size) for i in range(size)])


def across(value):
    return lax.ppermute(value, ("yh", "yl"), [(0, 3), (1, 2), (2, 1), (3, 0)])


def dot(left, right):
    return lax.dot_general(left, right, (((1,), (1,)), ((), ())), preferred_element_type=jnp.float32)


def assemble_kernel(place, *refs):
    *parts, out, held = refs
    yh, x, z = place[0], place[1], place[2]
    for d in range(4):
        for y in range(2):
            for part, at, group in ((parts[y * 4 + d], 0, GROUPS[0]), (parts[8 + d], y * PADDED, GROUPS[1])):
                for j, a in enumerate(group):
                    held[y * 4 + d, a, :, :ROWS] = part[at : at + PADDED, j * ROWS : (j + 1) * ROWS]
    for y in range(2):
        for i in range(4):
            source = lax.rem(y + yh, 2) * 4 + lax.rem(x - i + 4, 4)
            for a in range(8):
                at = ((y * 4 + i) * 8 + a) * ROWS
                out[:, at : at + ROWS] = held[source, lax.rem(a - z + 8, 8), :PIECE, :ROWS]


def assemble(place, parts):
    return pl.pallas_call(
        assemble_kernel,
        out_shape=jax.ShapeDtypeStruct((PIECE, 64 * ROWS), jnp.float32),
        in_specs=[pl.BlockSpec(memory_space=pltpu.SMEM)] + [pl.BlockSpec(memory_space=pltpu.VMEM)] * len(parts),
        out_specs=pl.BlockSpec(memory_space=pltpu.VMEM),
        scratch_shapes=[pltpu.VMEM((8, 8, PADDED, 256), jnp.float32)],
        compiler_params=pltpu.CompilerParams(vmem_limit_bytes=16 * 1024 * 1024),
    )(place, *parts)


def hold(*values):
    return lax.optimization_barrier(values)


def owner_order_kernel(place, *refs):
    *slices, out = refs
    yl, core = place[3], place[4]
    for k, rows in enumerate(slices):
        for y in range(2):
            slot = 2 * k + jnp.where(yl == y, 1, 0)
            for c in range(2):

                @pl.when(core == c)
                def _(at=(y * 2 + c) * PIECE):
                    out[slot, :PIECE] = rows[at : at + PIECE]

            out[slot, PIECE:] = jnp.zeros((PADDED - PIECE, DEPTH), rows.dtype)


def owner_order(place, *slices):
    return pl.pallas_call(
        owner_order_kernel,
        out_shape=jax.ShapeDtypeStruct((4, PADDED, DEPTH), slices[0].dtype),
        in_specs=[pl.BlockSpec(memory_space=pltpu.SMEM)] + [pl.BlockSpec(memory_space=pltpu.VMEM)] * 2,
        out_specs=pl.BlockSpec(memory_space=pltpu.VMEM),
        compiler_params=pltpu.CompilerParams(vmem_limit_bytes=12 * 1024 * 1024),
    )(place, *slices)


def left_rows(blocks, halves):
    pieces = [block.reshape(2, 2, PADDED, DEPTH) for block in blocks]
    return [jnp.concatenate([piece[k, half] for half in halves for piece in pieces]) for k in range(2)]


def product(left, right):
    total = dot(left[0], right[0]) + dot(left[1], right[1])
    return total[: 4 * PADDED], total[4 * PADDED :]


def both_cores(*blocks):
    joined = shift(jnp.concatenate(blocks), "c", 1)
    return [joined[i * ROWS : (i + 1) * ROWS] for i in range(len(blocks))]


def to_owner_x(value):
    rows = value.shape[0] // 4
    return [value[:rows]] + [shift(value[d * rows : (d + 1) * rows], "x", d) for d in range(1, 4)]


def on_device(blocks):
    place = jnp.stack([lax.axis_index(name) for name in ("yh", "x", "z", "yl", "c")]).astype(jnp.int32)
    own = blocks.reshape(ROWS, DEPTH)
    z1, z7 = shift(own, "z", -1), shift(own, "z", 1)
    (own_,) = both_cores(own)
    mine = owner_order(place, own, own_).reshape(4 * PADDED, DEPTH)

    x1, x3, other = shift(mine, "x", -1), shift(mine, "x", 1), shift(mine, "yh", 1)
    z1, z7 = hold(z1, z7)
    z2, z6 = shift(z1, "z", -1), shift(z7, "z", 1)
    x1, x3, other, z1, z7 = hold(x1, x3, other, z1, z7)
    ahead = shift(jnp.concatenate([x1[:HALF], other[HALF:]]), "x", -1)
    behind = shift(jnp.concatenate([other[:HALF], x3[HALF:]]), "x", 1)
    yh = shift(jnp.concatenate([x1[:HALF], x3[HALF:]]), "yh", 1)
    z2, z6, x1, x3 = hold(z2, z6, x1, x3)

    z3, z5 = shift(z2, "z", -1), shift(z6, "z", 1)
    ahead, behind, yh, z2, z6 = hold(ahead, behind, yh, z2, z6)
    o2_low, o2_high = shift(yh[:HALF], "x", -1), shift(yh[HALF:], "x", 1)
    pair_a, pair_b = hold(jnp.concatenate([z1, z7]), jnp.concatenate([z2, z6]))
    first = jnp.concatenate([pair_a, pair_b])
    first_ = shift(first, "c", 1)
    x2 = jnp.concatenate([ahead[:HALF], behind[HALF:]])
    o1 = jnp.concatenate([yh[:HALF], ahead[HALF:]])
    o3 = jnp.concatenate([behind[:HALF], yh[HALF:]])
    near = left_rows((mine, x1, x2, x3), (0, 1))
    first_, *near = hold(first_, *near)
    first = [jnp.concatenate([own, first]), jnp.concatenate([own_, first_])]
    n1, n1_kept = product(near, first)
    z3, z5, n1, near, first = hold(z3, z5, n1, tuple(near), tuple(first))

    n1 = shift(n1, "yl", 1)
    z4_low, z4_high = shift(z3[:80], "z", -1), shift(z5[80:], "z", 1)
    z3_, z5_ = both_cores(z3, z5)
    z3_, z5_, o2_low, o2_high = hold(z3_, z5_, o2_low, o2_high)
    far = left_rows((other, o1, jnp.concatenate([o2_low, o2_high]), o3), (1, 0))
    f1, f1_kept = product(far, first)
    z4_low, z4_high, f1, far = hold(z4_low, z4_high, f1, tuple(far))

    f1 = shift(f1, "yl", 1)
    z4 = jnp.concatenate([z4_low, z4_high])
    (z4_,) = both_cores(z4)
    z3_, z4_, z5_ = hold(z3_, z4_, z5_)
    last = [jnp.concatenate([z3, z4, z5]), jnp.concatenate([z3_, z4_, z5_])]
    f2, f2_kept = product(far, last)
    last, f2 = hold(tuple(last), f2)
    n2, n2_kept = product(near, last)
    n1, f2, n2 = hold(n1, f2, n2)

    n1_parts = to_owner_x(n1_kept + n1)
    f2 = shift(f2, "yl", 1)
    f1, n2, *n1_parts = hold(f1, n2, *n1_parts)

    n2 = shift(n2, "yl", 1)
    f1 = across(f1_kept + f1)
    f2, f1_kept = hold(f2, f1_kept)
    f2 = across(f2_kept + f2)
    f1, f2_kept = hold(f1, f2_kept)
    f1_parts = to_owner_x(f1)
    f2, n2, *f1_parts = hold(f2, n2, *f1_parts)

    second = jnp.concatenate([(n2_kept + n2).reshape(4, PADDED, -1), f2.reshape(4, PADDED, -1)], axis=1)
    second = to_owner_x(second.reshape(8 * PADDED, -1))
    return assemble(place, n1_parts + f1_parts + second)


def solution(mesh):
    finer = Mesh(mesh.devices.reshape(2, 4, 8, 2, 2), ("yh", "x", "z", "yl", "c"))
    return jax.shard_map(
        on_device,
        mesh=finer,
        in_specs=(P(("yh", "x", "z"), ("yl", "c"), None),),
        out_specs=P(("yh", "x", "z", "yl", "c"), None),
        check_vma=False,
    )
```

```python
import functools

import jax
import jax.numpy as jnp
from jax import lax
from jax.experimental import pallas as pl
from jax.experimental.pallas import tpu as pltpu
from jax.sharding import Mesh
from jax.sharding import PartitionSpec as P

ROWS = 152
DEPTH = 2400
PIECE = 38
PADDED = 40
HALF = 2 * PADDED
GROUPS = ((0, 1, 7, 2, 6), (3, 4, 5))


def shift(value, axis, by):
    size = lax.axis_size(axis)
    return lax.ppermute(value, axis, [(i, (i + by) % size) for i in range(size)])


def across(value):
    return lax.ppermute(value, ("yh", "yl"), [(0, 3), (1, 2), (2, 1), (3, 0)])


def dot(left, right):
    return lax.dot_general(left, right, (((1,), (1,)), ((), ())), preferred_element_type=jnp.float32)


def assemble_kernel(place, *refs):
    *parts, out, held = refs
    yh, x, z = place[0], place[1], place[2]
    for d in range(4):
        for y in range(2):
            for part, at, group in ((parts[y * 4 + d], 0, GROUPS[0]), (parts[8 + d], y * PADDED, GROUPS[1])):
                for j, a in enumerate(group):
                    held[y * 4 + d, a, :, :ROWS] = part[at : at + PADDED, j * ROWS : (j + 1) * ROWS]
    for y in range(2):
        for i in range(4):
            source = lax.rem(y + yh, 2) * 4 + lax.rem(x - i + 4, 4)
            for a in range(8):
                at = ((y * 4 + i) * 8 + a) * ROWS
                out[:, at : at + ROWS] = held[source, lax.rem(a - z + 8, 8), :PIECE, :ROWS]


def assemble(place, parts):
    return pl.pallas_call(
        assemble_kernel,
        out_shape=jax.ShapeDtypeStruct((PIECE, 64 * ROWS), jnp.float32),
        in_specs=[pl.BlockSpec(memory_space=pltpu.SMEM)] + [pl.BlockSpec(memory_space=pltpu.VMEM)] * len(parts),
        out_specs=pl.BlockSpec(memory_space=pltpu.VMEM),
        scratch_shapes=[pltpu.VMEM((8, 8, PADDED, 256), jnp.float32)],
        compiler_params=pltpu.CompilerParams(vmem_limit_bytes=16 * 1024 * 1024),
    )(place, *parts)


def hold(*values):
    return lax.optimization_barrier(values)


def owner_order_kernel(place, *refs):
    *slices, out = refs
    yl, core = place[3], place[4]
    for k, rows in enumerate(slices):
        for y in range(2):
            slot = 2 * k + jnp.where(yl == y, 1, 0)
            for c in range(2):

                @pl.when(core == c)
                def _(at=(y * 2 + c) * PIECE):
                    out[slot, :PIECE] = rows[at : at + PIECE]

            out[slot, PIECE:] = jnp.zeros((PADDED - PIECE, DEPTH), rows.dtype)


def owner_order(place, *slices):
    return pl.pallas_call(
        owner_order_kernel,
        out_shape=jax.ShapeDtypeStruct((4, PADDED, DEPTH), slices[0].dtype),
        in_specs=[pl.BlockSpec(memory_space=pltpu.SMEM)] + [pl.BlockSpec(memory_space=pltpu.VMEM)] * 2,
        out_specs=pl.BlockSpec(memory_space=pltpu.VMEM),
        compiler_params=pltpu.CompilerParams(vmem_limit_bytes=12 * 1024 * 1024),
    )(place, *slices)


def left_rows(blocks, halves):
    pieces = [block.reshape(2, 2, PADDED, DEPTH) for block in blocks]
    return [jnp.concatenate([piece[k, half] for half in halves for piece in pieces]) for k in range(2)]


def product(left, right):
    total = dot(left[0], right[0]) + dot(left[1], right[1])
    return total[: 4 * PADDED], total[4 * PADDED :]


def both_cores(*blocks):
    joined = shift(jnp.concatenate(blocks), "c", 1)
    return [joined[i * ROWS : (i + 1) * ROWS] for i in range(len(blocks))]


def to_owner_x(value):
    rows = value.shape[0] // 4
    return [value[:rows]] + [shift(value[d * rows : (d + 1) * rows], "x", d) for d in range(1, 4)]


def on_device(blocks):
    place = jnp.stack([lax.axis_index(name) for name in ("yh", "x", "z", "yl", "c")]).astype(jnp.int32)
    own = blocks.reshape(ROWS, DEPTH)
    z1, z7 = shift(own, "z", -1), shift(own, "z", 1)
    (own_,) = both_cores(own)
    mine = owner_order(place, own, own_).reshape(4 * PADDED, DEPTH)

    x1, x3, other = shift(mine, "x", -1), shift(mine, "x", 1), shift(mine, "yh", 1)
    z1, z7 = hold(z1, z7)
    z2, z6 = shift(z1, "z", -1), shift(z7, "z", 1)
    x1, x3, other, z1, z7 = hold(x1, x3, other, z1, z7)
    ahead = shift(jnp.concatenate([x1[:HALF], other[HALF:]]), "x", -1)
    behind = shift(jnp.concatenate([other[:HALF], x3[HALF:]]), "x", 1)
    yh = shift(jnp.concatenate([x1[:HALF], x3[HALF:]]), "yh", 1)
    z2, z6, x1, x3 = hold(z2, z6, x1, x3)

    z3, z5 = shift(z2, "z", -1), shift(z6, "z", 1)
    ahead, behind, yh, z2, z6 = hold(ahead, behind, yh, z2, z6)
    o2_low, o2_high = shift(yh[:HALF], "x", -1), shift(yh[HALF:], "x", 1)
    pair_a, pair_b = hold(jnp.concatenate([z1, z7]), jnp.concatenate([z2, z6]))
    first = jnp.concatenate([pair_a, pair_b])
    first_ = shift(first, "c", 1)
    x2 = jnp.concatenate([ahead[:HALF], behind[HALF:]])
    o1 = jnp.concatenate([yh[:HALF], ahead[HALF:]])
    o3 = jnp.concatenate([behind[:HALF], yh[HALF:]])
    near = left_rows((mine, x1, x2, x3), (0, 1))
    first_, *near = hold(first_, *near)
    first = [jnp.concatenate([own, first]), jnp.concatenate([own_, first_])]
    n1, n1_kept = product(near, first)
    z3, z5, n1, near, first = hold(z3, z5, n1, tuple(near), tuple(first))

    n1 = shift(n1, "yl", 1)
    z4_low, z4_high = shift(z3[:80], "z", -1), shift(z5[80:], "z", 1)
    z3_, z5_ = both_cores(z3, z5)
    z3_, z5_, o2_low, o2_high = hold(z3_, z5_, o2_low, o2_high)
    far = left_rows((other, o1, jnp.concatenate([o2_low, o2_high]), o3), (1, 0))
    f1, f1_kept = product(far, first)
    z4_low, z4_high, f1, far = hold(z4_low, z4_high, f1, tuple(far))

    f1 = shift(f1, "yl", 1)
    z4 = jnp.concatenate([z4_low, z4_high])
    (z4_,) = both_cores(z4)
    z3_, z4_, z5_ = hold(z3_, z4_, z5_)
    last = [jnp.concatenate([z3, z4, z5]), jnp.concatenate([z3_, z4_, z5_])]
    f2, f2_kept = product(far, last)
    last, f2 = hold(tuple(last), f2)
    n2, n2_kept = product(near, last)
    n1, f2, n2 = hold(n1, f2, n2)

    n1_parts = to_owner_x(n1_kept + n1)
    f2 = shift(f2, "yl", 1)
    f1, n2 = hold(f1, n2)

    n2 = shift(n2, "yl", 1)
    f1 = across(f1_kept + f1)
    f2, f1_kept, *n1_parts = hold(f2, f1_kept, *n1_parts)
    f2 = across(f2_kept + f2)
    f1, f2_kept = hold(f1, f2_kept)
    f1_parts = to_owner_x(f1)
    f2, n2, *f1_parts = hold(f2, n2, *f1_parts)

    second = jnp.concatenate([(n2_kept + n2).reshape(4, PADDED, -1), f2.reshape(4, PADDED, -1)], axis=1)
    second = to_owner_x(second.reshape(8 * PADDED, -1))
    return assemble(place, n1_parts + f1_parts + second)


def solution(mesh):
    finer = Mesh(mesh.devices.reshape(2, 4, 8, 2, 2), ("yh", "x", "z", "yl", "c"))
    return jax.shard_map(
        on_device,
        mesh=finer,
        in_specs=(P(("yh", "x", "z"), ("yl", "c"), None),),
        out_specs=P(("yh", "x", "z", "yl", "c"), None),
        check_vma=False,
    )
```
